32 devices in a mesh: grp: 2 (over x), wide: 8 (over z, y), narrow: 2 (over core).
Axes of the slice: x: 2, y: 2, z: 4, core: 2. Of those that a mesh axis runs over, the one named last changes fastest.
Arguments:
- tokens: bfloat16 [10240, 8192], P(('grp', 'wide'), 'narrow'), parts along dimension 0, may hold values from -6 to 6
- key_value_weight: bfloat16 [8192, 2048], P('narrow'), may hold values from -0.0625 to 0.0625
- adapter_down_weight: bfloat16 [8192, 64, 64], P('narrow', ('grp', 'wide')), parts along dimension 1, may hold values from -0.0625 to 0.0625
- adapter_up_weight: bfloat16 [64, 64, 2048], P(('grp', 'wide')), parts along dimension 0, may hold values from -0.75 to 0.75
- token_adapter_index: int32 [10240], P(('grp', 'wide')), parts along dimension 0, may hold values from 0 to 31, as said below
- adapter_rank_list: int32 [64], P(('grp', 'wide')), parts along dimension 0, may hold values from 16 to 64, as said below
Outputs:
- projected: bfloat16 [10240, 2048], P(('grp', 'wide'), 'narrow'), parts along dimension 0
The draws below stay inside these ranges and needn't reach their ends.
There are 2 independent parts, one for each index of `grp`. The reference program is written for one: setup_inputs(seed, part) draws one part's arguments, and reference() takes and returns one part's arrays. A program takes and returns all parts, laid end to end along the dimension named above; an argument that names none is the same for every part. Nothing has to cross between parts.
Inputs may be any that keep to these rules, and one draw needn't show every extreme that they name: `token_adapter_index`: tokens of one index of wide come in pieces of 16 that share an adapter. The adapters a with a // 4 = o belong to owner o; at most 128 tokens of one index of wide name adapters of one owner, and in every draw some owner gets exactly 128 tokens from every index of wide. `adapter_rank_list`: each rank is 64, 32 or 16.
All inputs are finite; a program needn't handle non-finite values.
Results may differ from the reference program's by a relative error of at most 0.006.
Values may be sent and summed in bfloat16 or wider, within the bound.
A program may use at most 192 MiB of HBM per device.

```python
import jax
import jax.numpy as jnp
from jax import lax

MODEL_WIDTH = 8192
KEY_VALUE_WIDTH = 2048
LARGEST_RANK = 64
ALPHA = 32
BLOCK = 128
PIECE = 16
ADP_DEV = 4
TOK_DEV = 640
ADAPTER_COUNT = 32
TOKENS = 5120
N_WIDE = 8


def draw_token_adapter_index(key, part):
    key = jax.random.fold_in(key, 7)
    hottest = jax.random.randint(jax.random.fold_in(key, 1), (), 0, N_WIDE, dtype=jnp.int32)
    per_owner = BLOCK // PIECE
    slot_count = (N_WIDE - 1) * per_owner
    picked = (TOK_DEV - BLOCK) // PIECE
    piece_count = TOK_DEV // PIECE

    def device_ident(device):
        device_key = jax.random.fold_in(key, 100 + device)
        first_key, second_key, third_key = jax.random.split(device_key, 3)
        scores = jax.random.randint(first_key, (slot_count,), 0, 1 << 16, dtype=jnp.int32) * slot_count + jnp.arange(slot_count, dtype=jnp.int32)
        larger = jnp.sum((scores[None, :] > scores[:, None]).astype(jnp.int32), axis=1)
        owner_rel = jnp.arange(slot_count, dtype=jnp.int32) // per_owner
        owner_abs = (hottest + 1 + owner_rel) % N_WIDE
        chosen = jnp.zeros((picked + 1,), jnp.int32).at[larger].set(owner_abs, mode='drop')
        piece_owner = jnp.concatenate([jnp.full((per_owner,), hottest, jnp.int32), chosen[:picked]])
        piece_owner = jax.random.permutation(second_key, piece_owner)
        portion_adapter = jax.random.randint(third_key, (piece_count,), 0, ADP_DEV, dtype=jnp.int32)
        return jnp.repeat(piece_owner * ADP_DEV + portion_adapter, PIECE, total_repeat_length=TOK_DEV)
    return jax.vmap(device_ident)(jnp.arange(N_WIDE, dtype=jnp.int32)).reshape(-1)


def draw_adapter_rank_list(key, part):
    key = jax.random.fold_in(key, 23)
    first_key, second_key, third_key = jax.random.split(key, 3)
    shifts = jax.random.randint(first_key, (ADAPTER_COUNT,), 0, 3, dtype=jnp.int32)
    result = jnp.right_shift(jnp.full((ADAPTER_COUNT,), LARGEST_RANK, jnp.int32), shifts)
    first_pos = jax.random.randint(second_key, (), 0, ADAPTER_COUNT, dtype=jnp.int32)
    second_pos = (first_pos + 1 + jax.random.randint(third_key, (), 0, ADAPTER_COUNT - 1, dtype=jnp.int32)) % ADAPTER_COUNT
    result = result.at[first_pos].set(LARGEST_RANK)
    return result.at[second_pos].set(LARGEST_RANK // 4)


def steps_of(rng, dims, cuts, smallest, top_value):
    def one(axis_at, parts):
        draws = jax.random.uniform(jax.random.fold_in(jax.random.fold_in(rng, 6), axis_at), (parts,), jnp.float32, smallest / len(cuts), top_value / len(cuts))
        return jnp.repeat(jnp.exp(draws), dims[axis_at] // parts).reshape((-1,) + (1,) * (len(dims) - axis_at - 1))

    factor_of = one(*cuts[0])
    for cut in cuts[1:]:
        factor_of = factor_of * one(*cut)
    return factor_of


def noise(rng, dims, width, most, cuts=(), kind=jnp.bfloat16):
    values = jax.random.normal(rng, dims, jnp.float32) * width
    if len(cuts) > 0:
        values = steps_of(rng, dims, cuts, -0.22, 0.18) * values
    return jnp.clip(values, min=-most, max=most).astype(kind)


def setup_inputs(seed: int = 0, part: int = 0) -> dict:
    streams_of = jax.random.split(jax.random.key(seed), 7)
    part_splits = jax.random.split(jax.random.fold_in(streams_of[6], part), 7)
    tokens = noise(part_splits[0], (TOKENS, MODEL_WIDTH), 1.0, 6.0, ((0, 8), (1, 2)))
    key_value_weight = noise(streams_of[1], (MODEL_WIDTH, KEY_VALUE_WIDTH), MODEL_WIDTH ** -0.5, 0.0625, ((0, 2),))
    adapter_down_weight = noise(part_splits[2], (MODEL_WIDTH, ADAPTER_COUNT, LARGEST_RANK), MODEL_WIDTH ** -0.5, 0.0625, ((0, 2), (1, 8)))
    adapter_up_weight = noise(part_splits[3], (ADAPTER_COUNT, LARGEST_RANK, KEY_VALUE_WIDTH), LARGEST_RANK ** -0.5, 0.75, ((0, 8),))
    token_adapter_index = draw_token_adapter_index(jax.random.fold_in(jax.random.fold_in(streams_of[6], part), 71), part)
    adapter_rank_list = draw_adapter_rank_list(jax.random.fold_in(jax.random.fold_in(streams_of[6], part), 71), part)
    return {"tokens": tokens, "key_value_weight": key_value_weight, "adapter_down_weight": adapter_down_weight, "adapter_up_weight": adapter_up_weight, "token_adapter_index": token_adapter_index, "adapter_rank_list": adapter_rank_list}


def reference(tokens, key_value_weight, adapter_down_weight, adapter_up_weight, token_adapter_index, adapter_rank_list):
    base_product = jnp.dot(tokens, key_value_weight, preferred_element_type=jnp.float32)
    overall_row_count = tokens.shape[0]
    block_row_list = 128
    row_padded_count = (overall_row_count + block_row_list - 1) // block_row_list * block_row_list
    extra_rows = row_padded_count - overall_row_count
    token_padding = jnp.pad(tokens, ((0, extra_rows), (0, 0)))
    identity_padding = jnp.pad(token_adapter_index, (0, extra_rows))

    def single_block(packed):
        block_tokens, block_identity = packed
        down_row_list = jnp.take(adapter_down_weight, block_identity, axis=1).astype(jnp.float32)
        shrink = jnp.einsum("td,dtr->tr", block_tokens.astype(jnp.float32), down_row_list, precision=lax.Precision.HIGHEST)
        rank_rows = jnp.take(adapter_rank_list, block_identity)
        kept_cols = jnp.arange(LARGEST_RANK, dtype=jnp.int32)[None, :] < rank_rows[:, None]
        coefficient = jnp.where(kept_cols, ALPHA / rank_rows.astype(jnp.float32)[:, None], jnp.float32(0.0))
        up_row_list = jnp.take(adapter_up_weight, block_identity, axis=0).astype(jnp.float32)
        return jnp.einsum("tr,trk->tk", shrink * coefficient, up_row_list, precision=lax.Precision.HIGHEST)

    adapter_correction = lax.map(single_block, (token_padding.reshape(-1, block_row_list, MODEL_WIDTH), identity_padding.reshape(-1, block_row_list)))
    adapter_correction = adapter_correction.reshape(row_padded_count, KEY_VALUE_WIDTH)[:overall_row_count]
    return (base_product + adapter_correction).astype(jnp.bfloat16)
```

```python
import jax
import jax.numpy as jnp
from jax import lax
from jax.sharding import PartitionSpec as P

ALPHA = 32


def local(
    tokens,
    key_value_weight,
    adapter_down_weight,
    adapter_up_weight,
    token_adapter_index,
    adapter_rank_list,
):
    narrow_count = lax.axis_size("narrow")
    narrow_index = lax.axis_index("narrow")
    rows, depth = tokens.shape
    local_count, rank_limit, width = adapter_up_weight.shape
    columns = local_count * rank_limit
    part = width // narrow_count
    down = adapter_down_weight.reshape(depth, columns)
    up = lax.dynamic_slice_in_dim(
        adapter_up_weight.reshape(columns, width), narrow_index * part, part, 1
    )
    all_down = lax.all_gather(down, "wide")
    all_up = lax.all_gather(up, "wide", tiled=True)
    all_rank = lax.all_gather(adapter_rank_list, "wide", tiled=True)
    adapters = all_rank.shape[0]

    base = jnp.dot(tokens, key_value_weight, preferred_element_type=jnp.float32)
    base = lax.psum_scatter(base, "narrow", scatter_dimension=1, tiled=True)

    same = token_adapter_index[:, None] == jnp.arange(adapters, dtype=jnp.int32)[None, :]
    shrink = jnp.einsum("td,wdc->twc", tokens, all_down, preferred_element_type=jnp.float32)
    shrink = shrink.reshape(rows, adapters, rank_limit)
    chosen = jnp.sum(jnp.where(same[:, :, None], shrink, jnp.float32(0.0)), axis=1)
    chosen = lax.psum(chosen, "narrow")
    rank = jnp.sum(jnp.where(same, all_rank[None, :], 0), axis=1)
    kept = jnp.arange(rank_limit, dtype=jnp.int32)[None, :] < rank[:, None]
    scaled = jnp.where(kept, chosen * (ALPHA / rank.astype(jnp.float32))[:, None], jnp.float32(0.0))
    spread = jnp.where(same[:, :, None], scaled[:, None, :], jnp.float32(0.0)).astype(jnp.bfloat16)
    adapted = jnp.dot(
        spread.reshape(rows, adapters * rank_limit), all_up, preferred_element_type=jnp.float32
    )
    return (base + adapted).astype(jnp.bfloat16)


def solution(mesh):
    in_specs = (
        P(("grp", "wide"), "narrow"),
        P("narrow", None),
        P("narrow", ("grp", "wide"), None),
        P(("grp", "wide"), None, None),
        P(("grp", "wide")),
        P(("grp", "wide")),
    )
    out_specs = P(("grp", "wide"), "narrow")
    return jax.shard_map(local, mesh=mesh, in_specs=in_specs, out_specs=out_specs, check_vma=False)
```

```python
import functools

import jax
import jax.numpy as jnp
from jax import lax
from jax.experimental import pallas as pl
from jax.experimental.pallas import tpu as pltpu
from jax.sharding import PartitionSpec as P

ALPHA = 32
MESH = pl.DeviceIdType.MESH
FIRST = 3


def chunks_of(slabs):
    main = slabs - FIRST
    size = main // 4
    ranges = [(FIRST + i * size, size if i < 3 else main - 3 * size) for i in range(4)]
    return ranges + [(0, FIRST)]


def kernel(
    wide_count,
    tokens_ref,
    weight_ref,
    block_ref,
    code_ref,
    out_ref,
    buf,
    tok,
    tile,
    part,
    got,
    upv,
    total,
    total_got,
    spread,
    tok_sem,
    tile_sem,
    up_sem,
    z_send,
    z_recv,
    y_send,
    y_recv,
    own_send,
    own_recv,
    n_send,
    n_recv,
):
    planes = wide_count // 2
    me = lax.axis_index("wide")
    core = lax.axis_index("narrow")
    z = me // 2
    y = me % 2
    partner = z * 2 + (1 - y)
    other = 1 - core
    slabs = block_ref.shape[0]
    depth_slabs = weight_ref.shape[0]
    slab = weight_ref.shape[1]
    tiles = weight_ref.shape[2] // slab
    half = tiles // 2
    chunks = chunks_of(slabs)
    main_count = len(chunks) - 1

    barrier = pltpu.get_barrier_semaphore()
    pl.semaphore_signal(barrier, inc=1, device_id={"wide": partner}, device_id_type=MESH)
    pl.semaphore_signal(barrier, inc=1, device_id={"narrow": other}, device_id_type=MESH)

    @pl.when(z > 0)
    def _():
        pl.semaphore_signal(barrier, inc=1, device_id={"wide": me - 2}, device_id_type=MESH)

    @pl.when(z < planes - 1)
    def _():
        pl.semaphore_signal(barrier, inc=1, device_id={"wide": me + 2}, device_id_type=MESH)

    peers = 2 + jnp.where(z > 0, 1, 0) + jnp.where(z < planes - 1, 1, 0)
    pl.semaphore_wait(barrier, peers)

    def z_copy(way, step, chunk, owner_z):
        if chunk < len(chunks):
            start, size = chunks[chunk]
            owner = owner_z * 2 + y
            source = block_ref if step == 1 else buf.at[owner]
        else:
            start, size = chunks[-1]
            owner = owner_z * 2 + (1 - y)
            source = buf.at[owner]
        return pltpu.make_async_remote_copy(
            src_ref=source.at[pl.ds(start, size)],
            dst_ref=buf.at[owner, pl.ds(start, size)],
            send_sem=z_send.at[way, step - 1, chunk],
            recv_sem=z_recv.at[way, step - 1, chunk],
            device_id={"wide": me + 2 if way == 0 else me - 2},
            device_id_type=MESH,
        )

    def y_copy(way, step, chunk, owner):
        start, size = chunks[chunk]
        return pltpu.make_async_remote_copy(
            src_ref=buf.at[owner, pl.ds(start, size)],
            dst_ref=buf.at[owner, pl.ds(start, size)],
            send_sem=y_send.at[way, step - 1, chunk],
            recv_sem=y_recv.at[way, step - 1, chunk],
            device_id={"wide": partner},
            device_id_type=MESH,
        )

    def own_copy(which, owner):
        start, size = (0, FIRST) if which == 0 else (FIRST, slabs - FIRST)
        return pltpu.make_async_remote_copy(
            src_ref=block_ref.at[pl.ds(start, size)],
            dst_ref=buf.at[owner, pl.ds(start, size)],
            send_sem=own_send.at[which],
            recv_sem=own_recv.at[which],
            device_id={"wide": partner},
            device_id_type=MESH,
        )

    def n_copy(source, target, which):
        return pltpu.make_async_remote_copy(
            src_ref=source,
            dst_ref=target,
            send_sem=n_send.at[which],
            recv_sem=n_recv.at[which],
            device_id={"narrow": other},
            device_id_type=MESH,
        )

    def can_send(way):
        return z < planes - 1 if way == 0 else z > 0

    def arrives(way, step):
        return z >= step if way == 0 else z + step <= planes - 1

    def forwards(way, step):
        return jnp.logical_and(arrives(way, step), can_send(way))

    def plane_of(way, step):
        return z - step if way == 0 else z + step

    load_tokens = pltpu.make_async_copy(tokens_ref, tok, tok_sem)
    load_tokens.start()
    own_copy(0, me).start()
    for chunk in range(len(chunks)):
        for way in range(2):

            @pl.when(can_send(way))
            def _(way=way, chunk=chunk):
                z_copy(way, 1, chunk, z).start()

    own_copy(1, me).start()
    own_copy(0, partner).wait_recv()
    for way in range(2):

        @pl.when(can_send(way))
        def _(way=way):
            z_copy(way, 1, len(chunks), z).start()

    def weight_load(step, slot):
        column = jnp.where(step < half, other * half + step, core * half + step - half)
        return pltpu.make_async_copy(
            weight_ref.at[:, :, pl.ds(pl.multiple_of(column * slab, slab), slab)],
            tile.at[slot],
            tile_sem.at[slot],
        )

    def product(slot):
        value = None
        group = 4
        def body(k, carry):
            offset = pl.multiple_of(k * (group * slab), group * slab)
            left = tok[:, pl.ds(offset, group * slab)]
            right = tile[slot, pl.ds(k * group, group)].reshape(group * slab, slab)
            return carry + jnp.dot(left, right, preferred_element_type=jnp.float32)

        zero = jnp.zeros((tok.shape[0], slab), jnp.float32)
        return lax.fori_loop(0, depth_slabs // group, body, zero)

    weight_load(0, 0).start()
    load_tokens.wait()

    def base_step(step, carry):
        slot = step % 2

        @pl.when(step < tiles - 1)
        def _():
            weight_load(step + 1, 1 - slot).start()

        weight_load(step, slot).wait()
        part[step] = product(slot)

        return carry

    lax.fori_loop(0, tiles, base_step, 0)
    base_copy = n_copy(part.at[pl.ds(0, half)], got, 0)
    base_copy.start()

    total[...] = jnp.zeros_like(total)

    def shrink(source, owner):
        down = pltpu.make_async_copy(source.at[pl.ds(0, depth_slabs)], tile.at[0], tile_sem.at[0])
        up = pltpu.make_async_copy(
            source.at[pl.ds(depth_slabs, slabs - depth_slabs)], upv.at[:, owner], up_sem
        )
        down.start()
        up.start()
        down.wait()
        up.wait()
        total[...] += jnp.where(code_ref[...] == owner, product(0), jnp.float32(0.0))

    shrink(block_ref, me)

    def across(step):
        for way in range(2):

            @pl.when(arrives(way, step))
            def _(way=way):
                owner = plane_of(way, step) * 2 + (1 - y)
                for chunk in range(main_count):
                    y_copy(way, step, chunk, owner).wait_recv()
                shrink(buf.at[owner], owner)

    for step in range(1, planes):
        for chunk in range(len(chunks) + 1):
            for way in range(2):

                @pl.when(arrives(way, step))
                def _(way=way, chunk=chunk):
                    plane = plane_of(way, step)
                    z_copy(way, step, chunk, plane).wait_recv()
                    if chunk < main_count:
                        y_copy(way, step, chunk, plane * 2 + y).start()

                if step < planes - 1:

                    @pl.when(forwards(way, step))
                    def _(way=way, chunk=chunk):
                        z_copy(way, step + 1, chunk, plane_of(way, step)).start()

        for way in range(2):

            @pl.when(arrives(way, step))
            def _(way=way):
                owner = plane_of(way, step) * 2 + y
                shrink(buf.at[owner], owner)

        if step == 1:
            own_copy(1, partner).wait_recv()
            shrink(buf.at[partner], partner)
        else:
            across(step - 1)
    across(planes - 1)

    total_copy = n_copy(total, total_got, 1)
    total_copy.start()
    total_copy.wait_recv()
    whole = total[...] + total_got[...]
    for owner in range(wide_count):
        spread[:, owner * slab : (owner + 1) * slab] = jnp.where(
            code_ref[...] == owner, whole, jnp.float32(0.0)
        ).astype(jnp.bfloat16)
    base_copy.wait_recv()

    def finish(i, carry):
        right = upv[i].reshape(wide_count * slab, slab)
        adapted = jnp.dot(spread[...], right, preferred_element_type=jnp.float32)
        value = part[half + i] + got[i] + adapted
        out_ref[:, pl.ds(pl.multiple_of(i * slab, slab), slab)] = value.astype(jnp.bfloat16)
        return carry

    lax.fori_loop(0, half, finish, 0)

    base_copy.wait_send()
    total_copy.wait_send()
    for which in range(2):
        own_copy(which, me).wait_send()
    for step in range(1, planes):
        for way in range(2):
            sends = can_send(way) if step == 1 else forwards(way, step - 1)

            @pl.when(sends)
            def _(way=way, step=step):
                for chunk in range(len(chunks) + 1):
                    z_copy(way, step, chunk, plane_of(way, step - 1)).wait_send()

            @pl.when(arrives(way, step))
            def _(way=way, step=step):
                for chunk in range(main_count):
                    y_copy(way, step, chunk, plane_of(way, step) * 2 + y).wait_send()


def local(
    tokens,
    key_value_weight,
    adapter_down_weight,
    adapter_up_weight,
    token_adapter_index,
    adapter_rank_list,
):
    wide_count = lax.axis_size("wide")
    narrow_count = lax.axis_size("narrow")
    narrow_index = lax.axis_index("narrow")
    rows, depth = tokens.shape
    local_count, rank_limit, width = adapter_up_weight.shape
    columns = local_count * rank_limit
    part = width // narrow_count
    depth_slabs = depth // columns
    part_slabs = part // columns
    slabs = depth_slabs + part_slabs
    planes = wide_count // 2

    up = lax.dynamic_slice_in_dim(adapter_up_weight, narrow_index * part, part, 2)
    rank = adapter_rank_list[:, None]
    kept = jnp.arange(rank_limit, dtype=jnp.int32)[None, :] < rank
    scale = jnp.where(kept, ALPHA / rank.astype(jnp.float32), jnp.float32(0.0))
    up = (up.astype(jnp.float32) * scale[:, :, None]).astype(jnp.bfloat16)
    up = up.reshape(columns, part_slabs, columns).transpose(1, 0, 2)
    block = jnp.concatenate([adapter_down_weight.reshape(depth_slabs, columns, columns), up], axis=0)
    column_adapter = jnp.arange(columns, dtype=jnp.int32) // rank_limit
    code = jnp.where(
        (token_adapter_index % local_count)[:, None] == column_adapter[None, :],
        (token_adapter_index // local_count)[:, None],
        -1,
    )

    any_space = pl.BlockSpec(memory_space=pl.ANY)
    vmem = pl.BlockSpec(memory_space=pltpu.VMEM)
    dma = pltpu.SemaphoreType.DMA
    out, _ = pl.pallas_call(
        functools.partial(kernel, wide_count),
        out_shape=(
            jax.ShapeDtypeStruct((rows, part), jnp.bfloat16),
            jax.ShapeDtypeStruct((wide_count, slabs, columns, columns), jnp.bfloat16),
        ),
        in_specs=[any_space, any_space, any_space, vmem],
        out_specs=(vmem, any_space),
        scratch_shapes=[
            pltpu.VMEM((rows, depth), jnp.bfloat16),
            pltpu.VMEM((2, depth_slabs, columns, columns), jnp.bfloat16),
            pltpu.VMEM((2 * part_slabs, rows, columns), jnp.float32),
            pltpu.VMEM((part_slabs, rows, columns), jnp.float32),
            pltpu.VMEM((part_slabs, wide_count, columns, columns), jnp.bfloat16),
            pltpu.VMEM((rows, columns), jnp.float32),
            pltpu.VMEM((rows, columns), jnp.float32),
            pltpu.VMEM((rows, wide_count * columns), jnp.bfloat16),
            dma,
            dma((2,)),
            dma,
            dma((2, planes - 1, 6)),
            dma((2, planes - 1, 6)),
            dma((2, planes - 1, 4)),
            dma((2, planes - 1, 4)),
            dma((2,)),
            dma((2,)),
            dma((2,)),
            dma((2,)),
        ],
        compiler_params=pltpu.CompilerParams(
            collective_id=0, has_side_effects=True, vmem_limit_bytes=56 * 1024 * 1024
        ),
    )(tokens, key_value_weight.reshape(depth_slabs, columns, width), block, code)
    return out


def solution(mesh):
    in_specs = (
        P(("grp", "wide"), "narrow"),
        P("narrow", None),
        P("narrow", ("grp", "wide"), None),
        P(("grp", "wide"), None, None),
        P(("grp", "wide")),
        P(("grp", "wide")),
    )
    out_specs = P(("grp", "wide"), "narrow")
    return jax.shard_map(local, mesh=mesh, in_specs=in_specs, out_specs=out_specs, check_vma=False)
```

```python
import functools

import jax
import jax.numpy as jnp
from jax import lax
from jax.experimental import pallas as pl
from jax.experimental.pallas import tpu as pltpu
from jax.sharding import PartitionSpec as P

ALPHA = 32
MESH = pl.DeviceIdType.MESH
FIRST = 3


def chunks_of(down_slabs, slabs):
    main = down_slabs - FIRST
    size = main // 3
    ranges = [(FIRST + i * size, size if i < 2 else main - 2 * size) for i in range(3)]
    return ranges + [(down_slabs, slabs - down_slabs), (0, FIRST)]


def kernel(
    wide_count,
    tokens_ref,
    weight_ref,
    down_ref,
    up_ref,
    code_ref,
    out_ref,
    buf,
    tok,
    tile,
    down_tile,
    part,
    got,
    upv,
    total,
    total_got,
    spread,
    tok_sem,
    tile_sem,
    up_sem,
    z_send,
    z_recv,
    y_send,
    y_recv,
    own_send,
    own_recv,
    n_send,
    n_recv,
):
    planes = wide_count // 2
    me = lax.axis_index("wide")
    core = lax.axis_index("narrow")
    z = me // 2
    y = me % 2
    partner = z * 2 + (1 - y)
    other = 1 - core
    down_slabs = down_ref.shape[0]
    slabs = down_slabs + up_ref.shape[0]
    depth_slabs = weight_ref.shape[0]
    depth = down_ref.shape[2]
    slab = weight_ref.shape[1]
    tiles = weight_ref.shape[2] // slab
    half = tiles // 2
    chunks = chunks_of(down_slabs, slabs)
    main_count = len(chunks) - 1

    def mine(start, size):
        if start < down_slabs:
            return down_ref.at[pl.ds(start, size)]
        return up_ref.at[pl.ds(start - down_slabs, size)]


    barrier = pltpu.get_barrier_semaphore()
    pl.semaphore_signal(barrier, inc=1, device_id={"wide": partner}, device_id_type=MESH)
    pl.semaphore_signal(barrier, inc=1, device_id={"narrow": other}, device_id_type=MESH)

    @pl.when(z > 0)
    def _():
        pl.semaphore_signal(barrier, inc=1, device_id={"wide": me - 2}, device_id_type=MESH)

    @pl.when(z < planes - 1)
    def _():
        pl.semaphore_signal(barrier, inc=1, device_id={"wide": me + 2}, device_id_type=MESH)

    peers = 2 + jnp.where(z > 0, 1, 0) + jnp.where(z < planes - 1, 1, 0)
    pl.semaphore_wait(barrier, peers)

    def z_copy(way, step, chunk, owner_z):
        if chunk < len(chunks):
            start, size = chunks[chunk]
            owner = owner_z * 2 + y
            source = mine(start, size) if step == 1 else buf.at[owner, pl.ds(start, size)]
        else:
            start, size = chunks[-1]
            owner = owner_z * 2 + (1 - y)
            source = buf.at[owner, pl.ds(start, size)]
        return pltpu.make_async_remote_copy(
            src_ref=source,
            dst_ref=buf.at[owner, pl.ds(start, size)],
            send_sem=z_send.at[way, step - 1, chunk],
            recv_sem=z_recv.at[way, step - 1, chunk],
            device_id={"wide": me + 2 if way == 0 else me - 2},
            device_id_type=MESH,
        )

    def y_copy(way, step, chunk, owner):
        start, size = chunks[chunk]
        return pltpu.make_async_remote_copy(
            src_ref=buf.at[owner, pl.ds(start, size)],
            dst_ref=buf.at[owner, pl.ds(start, size)],
            send_sem=y_send.at[way, step - 1, chunk],
            recv_sem=y_recv.at[way, step - 1, chunk],
            device_id={"wide": partner},
            device_id_type=MESH,
        )

    def own_copy(which, owner):
        start, size = (
            (0, FIRST),
            (FIRST, down_slabs - FIRST),
            (down_slabs, slabs - down_slabs),
        )[which]
        return pltpu.make_async_remote_copy(
            src_ref=mine(start, size),
            dst_ref=buf.at[owner, pl.ds(start, size)],
            send_sem=own_send.at[which],
            recv_sem=own_recv.at[which],
            device_id={"wide": partner},
            device_id_type=MESH,
        )

    def n_copy(source, target, which):
        return pltpu.make_async_remote_copy(
            src_ref=source,
            dst_ref=target,
            send_sem=n_send.at[which],
            recv_sem=n_recv.at[which],
            device_id={"narrow": other},
            device_id_type=MESH,
        )

    def can_send(way):
        return z < planes - 1 if way == 0 else z > 0

    def arrives(way, step):
        return z >= step if way == 0 else z + step <= planes - 1

    def forwards(way, step):
        return jnp.logical_and(arrives(way, step), can_send(way))

    def plane_of(way, step):
        return z - step if way == 0 else z + step

    load_tokens = pltpu.make_async_copy(tokens_ref, tok, tok_sem)
    load_tokens.start()
    own_copy(0, me).start()
    for chunk in range(len(chunks)):
        for way in range(2):

            @pl.when(can_send(way))
            def _(way=way, chunk=chunk):
                z_copy(way, 1, chunk, z).start()

    own_copy(1, me).start()
    own_copy(2, me).start()
    own_copy(0, partner).wait_recv()
    for way in range(2):

        @pl.when(can_send(way))
        def _(way=way):
            z_copy(way, 1, len(chunks), z).start()

    def weight_load(step, slot):
        column = jnp.where(step < half, other * half + step, core * half + step - half)
        return pltpu.make_async_copy(
            weight_ref.at[:, :, pl.ds(pl.multiple_of(column * slab, slab), slab)],
            tile.at[slot],
            tile_sem.at[slot],
        )

    def product(slot):
        value = None
        group = 4
        def body(k, carry):
            offset = pl.multiple_of(k * (group * slab), group * slab)
            left = tok[:, pl.ds(offset, group * slab)]
            right = tile[slot, pl.ds(k * group, group)].reshape(group * slab, slab)
            return carry + jnp.dot(left, right, preferred_element_type=jnp.float32)

        zero = jnp.zeros((tok.shape[0], slab), jnp.float32)
        return lax.fori_loop(0, depth_slabs // group, body, zero)

    weight_load(0, 0).start()
    load_tokens.wait()

    def base_step(step, carry):
        slot = step % 2

        @pl.when(step < tiles - 1)
        def _():
            weight_load(step + 1, 1 - slot).start()

        weight_load(step, slot).wait()
        part[step] = product(slot)

        return carry

    lax.fori_loop(0, tiles, base_step, 0)
    base_copy = n_copy(part.at[pl.ds(0, half)], got, 0)
    base_copy.start()

    total[...] = jnp.zeros_like(total)

    def down_product():
        size = depth // 4

        def body(k, carry):
            offset = pl.multiple_of(k * size, size)
            left = tok[:, pl.ds(offset, size)]
            right = down_tile[:, :, pl.ds(offset, size)].reshape(slab, size)
            return carry + lax.dot_general(
                left, right, (((1,), (1,)), ((), ())), preferred_element_type=jnp.float32
            )

        zero = jnp.zeros((tok.shape[0], slab), jnp.float32)
        return lax.fori_loop(0, 4, body, zero)

    def shrink(down_source, up_source, owner):
        groups = upv.shape[1]
        width = upv.shape[4]
        down = pltpu.make_async_copy(down_source, down_tile, tile_sem.at[0])
        down.start()
        ups = [
            pltpu.make_async_copy(
                up_source.at[:, :, pl.ds(g * width, width)], upv.at[owner, g], up_sem.at[g]
            )
            for g in range(groups)
        ]
        for up in ups:
            up.start()
        down.wait()
        total[...] += jnp.where(code_ref[...] == owner, down_product(), jnp.float32(0.0))
        for up in ups:
            up.wait()

    shrink(down_ref, up_ref, me)

    def arrived(owner):
        shrink(
            buf.at[owner, pl.ds(0, down_slabs)],
            buf.at[owner, pl.ds(down_slabs, slabs - down_slabs)],
            owner,
        )

    def across(step):
        for way in range(2):

            @pl.when(arrives(way, step))
            def _(way=way):
                owner = plane_of(way, step) * 2 + (1 - y)
                for chunk in range(main_count):
                    y_copy(way, step, chunk, owner).wait_recv()
                arrived(owner)

    for step in range(1, planes):
        for chunk in range(len(chunks) + 1):
            for way in range(2):

                @pl.when(arrives(way, step))
                def _(way=way, chunk=chunk):
                    plane = plane_of(way, step)
                    z_copy(way, step, chunk, plane).wait_recv()
                    if chunk < main_count:
                        y_copy(way, step, chunk, plane * 2 + y).start()

                if step < planes - 1:

                    @pl.when(forwards(way, step))
                    def _(way=way, chunk=chunk):
                        z_copy(way, step + 1, chunk, plane_of(way, step)).start()

        for way in range(2):

            @pl.when(arrives(way, step))
            def _(way=way):
                owner = plane_of(way, step) * 2 + y
                arrived(owner)

        if step == 1:
            own_copy(1, partner).wait_recv()
            own_copy(2, partner).wait_recv()
            arrived(partner)
        else:
            across(step - 1)
    across(planes - 1)

    total_copy = n_copy(total, total_got, 1)
    total_copy.start()
    total_copy.wait_recv()
    whole = total[...] + total_got[...]
    for owner in range(wide_count):
        spread[:, owner * slab : (owner + 1) * slab] = jnp.where(
            code_ref[...] == owner, whole, jnp.float32(0.0)
        ).astype(jnp.bfloat16)
    base_copy.wait_recv()

    def finish(i, carry):
        columns = pl.ds(pl.multiple_of(i * slab, slab), slab)
        right = upv[:, :, :, :, columns].reshape(wide_count * slab, slab)
        adapted = jnp.dot(spread[...], right, preferred_element_type=jnp.float32)
        value = part[half + i] + got[i] + adapted
        out_ref[:, columns] = value.astype(jnp.bfloat16)
        return carry

    lax.fori_loop(0, half, finish, 0)

    base_copy.wait_send()
    total_copy.wait_send()
    for which in range(3):
        own_copy(which, me).wait_send()
    for step in range(1, planes):
        for way in range(2):
            sends = can_send(way) if step == 1 else forwards(way, step - 1)

            @pl.when(sends)
            def _(way=way, step=step):
                for chunk in range(len(chunks) + 1):
                    z_copy(way, step, chunk, plane_of(way, step - 1)).wait_send()

            @pl.when(arrives(way, step))
            def _(way=way, step=step):
                for chunk in range(main_count):
                    y_copy(way, step, chunk, plane_of(way, step) * 2 + y).wait_send()


def local(
    tokens,
    key_value_weight,
    adapter_down_weight,
    adapter_up_weight,
    token_adapter_index,
    adapter_rank_list,
):
    wide_count = lax.axis_size("wide")
    narrow_count = lax.axis_size("narrow")
    narrow_index = lax.axis_index("narrow")
    rows, depth = tokens.shape
    local_count, rank_limit, width = adapter_up_weight.shape
    columns = local_count * rank_limit
    part = width // narrow_count
    depth_slabs = depth // columns
    part_slabs = part // columns
    sub = 16
    down_slabs = columns // sub
    groups = depth // part
    up_rows = columns // groups
    up_slabs = up_rows // sub
    slabs = down_slabs + up_slabs
    planes = wide_count // 2

    up = lax.dynamic_slice_in_dim(adapter_up_weight, narrow_index * part, part, 2)
    rank = adapter_rank_list[:, None]
    kept = jnp.arange(rank_limit, dtype=jnp.int32)[None, :] < rank
    scale = jnp.where(kept, ALPHA / rank.astype(jnp.float32), jnp.float32(0.0))
    up = (up.astype(jnp.float32) * scale[:, :, None]).astype(jnp.bfloat16)
    up = up.reshape(groups, up_rows, part).transpose(1, 0, 2).reshape(up_slabs, sub, depth)
    down = adapter_down_weight.transpose(1, 2, 0).reshape(down_slabs, sub, depth)
    column_adapter = jnp.arange(columns, dtype=jnp.int32) // rank_limit
    code = jnp.where(
        (token_adapter_index % local_count)[:, None] == column_adapter[None, :],
        (token_adapter_index // local_count)[:, None],
        -1,
    )

    any_space = pl.BlockSpec(memory_space=pl.ANY)
    vmem = pl.BlockSpec(memory_space=pltpu.VMEM)
    dma = pltpu.SemaphoreType.DMA
    out, _ = pl.pallas_call(
        functools.partial(kernel, wide_count),
        out_shape=(
            jax.ShapeDtypeStruct((rows, part), jnp.bfloat16),
            jax.ShapeDtypeStruct((wide_count, slabs, sub, depth), jnp.bfloat16),
        ),
        in_specs=[any_space, any_space, any_space, any_space, vmem],
        out_specs=(vmem, any_space),
        scratch_shapes=[
            pltpu.VMEM((rows, depth), jnp.bfloat16),
            pltpu.VMEM((2, depth_slabs, columns, columns), jnp.bfloat16),
            pltpu.VMEM((down_slabs, sub, depth), jnp.bfloat16),
            pltpu.VMEM((2 * part_slabs, rows, columns), jnp.float32),
            pltpu.VMEM((part_slabs, rows, columns), jnp.float32),
            pltpu.VMEM((wide_count, groups, up_slabs, sub, part), jnp.bfloat16),
            pltpu.VMEM((rows, columns), jnp.float32),
            pltpu.VMEM((rows, columns), jnp.float32),
            pltpu.VMEM((rows, wide_count * columns), jnp.bfloat16),
            dma,
            dma((2,)),
            dma((groups,)),
            dma((2, planes - 1, 6)),
            dma((2, planes - 1, 6)),
            dma((2, planes - 1, 4)),
            dma((2, planes - 1, 4)),
            dma((3,)),
            dma((3,)),
            dma((2,)),
            dma((2,)),
        ],
        compiler_params=pltpu.CompilerParams(
            collective_id=0, has_side_effects=True, vmem_limit_bytes=56 * 1024 * 1024
        ),
    )(tokens, key_value_weight.reshape(depth_slabs, columns, width), down, up, code)
    return out


def solution(mesh):
    in_specs = (
        P(("grp", "wide"), "narrow"),
        P("narrow", None),
        P("narrow", ("grp", "wide"), None),
        P(("grp", "wide"), None, None),
        P(("grp", "wide")),
        P(("grp", "wide")),
    )
    out_specs = P(("grp", "wide"), "narrow")
    return jax.shard_map(local, mesh=mesh, in_specs=in_specs, out_specs=out_specs, check_vma=False)
```

```python
import functools

import jax
import jax.numpy as jnp
from jax import lax
from jax.experimental import pallas as pl
from jax.experimental.pallas import tpu as pltpu
from jax.sharding import PartitionSpec as P

ALPHA = 32
MESH = pl.DeviceIdType.MESH
FIRST = 3


def chunks_of(down_slabs):
    main = down_slabs - FIRST
    size = main // 3
    ranges = [(FIRST + i * size, size if i < 2 else main - 2 * size) for i in range(3)]
    return ranges + [(down_slabs, 0), (0, FIRST)]


def kernel(
    wide_count,
    tokens_ref,
    weight_ref,
    down_ref,
    up_ref,
    code_ref,
    out_ref,
    buf,
    up_buf,
    tok,
    tile,
    down_tile,
    part,
    got,
    upv,
    total,
    total_got,
    spread,
    tok_sem,
    tile_sem,
    up_sem,
    z_send,
    z_recv,
    y_send,
    y_recv,
    own_send,
    own_recv,
    n_send,
    n_recv,
):
    planes = wide_count // 2
    me = lax.axis_index("wide")
    core = lax.axis_index("narrow")
    z = me // 2
    y = me % 2
    partner = z * 2 + (1 - y)
    other = 1 - core
    down_slabs = down_ref.shape[0]
    up_at = down_slabs
    depth_slabs = weight_ref.shape[0]
    depth = down_ref.shape[2]
    slab = weight_ref.shape[1]
    tiles = weight_ref.shape[2] // slab
    half = tiles // 2
    chunks = chunks_of(down_slabs)
    main_count = len(chunks) - 1

    def mine(start, size):
        if start < down_slabs:
            return down_ref.at[pl.ds(start, size)]
        return up_ref

    def held(owner, start, size):
        if start < down_slabs:
            return buf.at[owner, pl.ds(start, size)]
        return up_buf.at[owner]


    barrier = pltpu.get_barrier_semaphore()
    pl.semaphore_signal(barrier, inc=1, device_id={"wide": partner}, device_id_type=MESH)
    pl.semaphore_signal(barrier, inc=1, device_id={"narrow": other}, device_id_type=MESH)

    @pl.when(z > 0)
    def _():
        pl.semaphore_signal(barrier, inc=1, device_id={"wide": me - 2}, device_id_type=MESH)

    @pl.when(z < planes - 1)
    def _():
        pl.semaphore_signal(barrier, inc=1, device_id={"wide": me + 2}, device_id_type=MESH)

    peers = 2 + jnp.where(z > 0, 1, 0) + jnp.where(z < planes - 1, 1, 0)
    pl.semaphore_wait(barrier, peers)

    def z_copy(way, step, chunk, owner_z):
        if chunk < len(chunks):
            start, size = chunks[chunk]
            owner = owner_z * 2 + y
            source = mine(start, size) if step == 1 else held(owner, start, size)
        else:
            start, size = chunks[-1]
            owner = owner_z * 2 + (1 - y)
            source = buf.at[owner, pl.ds(start, size)]
        return pltpu.make_async_remote_copy(
            src_ref=source,
            dst_ref=held(owner, start, size),
            send_sem=z_send.at[way, step - 1, chunk],
            recv_sem=z_recv.at[way, step - 1, chunk],
            device_id={"wide": me + 2 if way == 0 else me - 2},
            device_id_type=MESH,
        )

    def y_copy(way, step, chunk, owner):
        start, size = chunks[chunk]
        return pltpu.make_async_remote_copy(
            src_ref=held(owner, start, size),
            dst_ref=held(owner, start, size),
            send_sem=y_send.at[way, step - 1, chunk],
            recv_sem=y_recv.at[way, step - 1, chunk],
            device_id={"wide": partner},
            device_id_type=MESH,
        )

    def own_copy(which, owner):
        start, size = (
            (0, FIRST),
            (FIRST, down_slabs - FIRST),
            (up_at, 0),
        )[which]
        return pltpu.make_async_remote_copy(
            src_ref=mine(start, size),
            dst_ref=held(owner, start, size),
            send_sem=own_send.at[which],
            recv_sem=own_recv.at[which],
            device_id={"wide": partner},
            device_id_type=MESH,
        )

    def n_copy(source, target, which):
        return pltpu.make_async_remote_copy(
            src_ref=source,
            dst_ref=target,
            send_sem=n_send.at[which],
            recv_sem=n_recv.at[which],
            device_id={"narrow": other},
            device_id_type=MESH,
        )

    def can_send(way):
        return z < planes - 1 if way == 0 else z > 0

    def arrives(way, step):
        return z >= step if way == 0 else z + step <= planes - 1

    def forwards(way, step):
        return jnp.logical_and(arrives(way, step), can_send(way))

    def plane_of(way, step):
        return z - step if way == 0 else z + step

    load_tokens = pltpu.make_async_copy(tokens_ref, tok, tok_sem)
    load_tokens.start()
    own_copy(0, me).start()
    for chunk in range(len(chunks)):
        for way in range(2):

            @pl.when(can_send(way))
            def _(way=way, chunk=chunk):
                z_copy(way, 1, chunk, z).start()

    own_copy(1, me).start()
    own_copy(2, me).start()
    own_copy(0, partner).wait_recv()
    for way in range(2):

        @pl.when(can_send(way))
        def _(way=way):
            z_copy(way, 1, len(chunks), z).start()

    def weight_load(step, slot):
        column = jnp.where(step < half, other * half + step, core * half + step - half)
        return pltpu.make_async_copy(
            weight_ref.at[:, :, pl.ds(pl.multiple_of(column * slab, slab), slab)],
            tile.at[slot],
            tile_sem.at[slot],
        )

    def product(slot):
        value = None
        group = 4
        def body(k, carry):
            offset = pl.multiple_of(k * (group * slab), group * slab)
            left = tok[:, pl.ds(offset, group * slab)]
            right = tile[slot, pl.ds(k * group, group)].reshape(group * slab, slab)
            return carry + jnp.dot(left, right, preferred_element_type=jnp.float32)

        zero = jnp.zeros((tok.shape[0], slab), jnp.float32)
        return lax.fori_loop(0, depth_slabs // group, body, zero)

    weight_load(0, 0).start()
    load_tokens.wait()

    def base_step(step, carry):
        slot = step % 2

        @pl.when(step < tiles - 1)
        def _():
            weight_load(step + 1, 1 - slot).start()

        weight_load(step, slot).wait()
        part[step] = product(slot)

        return carry

    lax.fori_loop(0, tiles, base_step, 0)
    base_copy = n_copy(part.at[pl.ds(0, half)], got, 0)
    base_copy.start()

    total[...] = jnp.zeros_like(total)

    def down_product():
        size = depth // 4

        def body(k, carry):
            offset = pl.multiple_of(k * size, size)
            left = tok[:, pl.ds(offset, size)]
            right = down_tile[:, :, pl.ds(offset, size)].reshape(slab, size)
            return carry + lax.dot_general(
                left, right, (((1,), (1,)), ((), ())), preferred_element_type=jnp.float32
            )

        zero = jnp.zeros((tok.shape[0], slab), jnp.float32)
        return lax.fori_loop(0, 4, body, zero)

    def shrink(down_source, up_source, owner):
        down = pltpu.make_async_copy(down_source, down_tile, tile_sem.at[0])
        down.start()
        up = pltpu.make_async_copy(up_source, upv.at[owner], up_sem)
        up.start()
        down.wait()
        total[...] += jnp.where(code_ref[...] == owner, down_product(), jnp.float32(0.0))
        up.wait()

    shrink(down_ref, up_ref, me)

    def arrived(owner):
        shrink(
            buf.at[owner, pl.ds(0, down_slabs)],
            up_buf.at[owner],
            owner,
        )

    def across(step):
        for way in range(2):

            @pl.when(arrives(way, step))
            def _(way=way):
                owner = plane_of(way, step) * 2 + (1 - y)
                for chunk in range(main_count):
                    y_copy(way, step, chunk, owner).wait_recv()
                arrived(owner)

    for step in range(1, planes):
        for chunk in range(len(chunks) + 1):
            for way in range(2):

                @pl.when(arrives(way, step))
                def _(way=way, chunk=chunk):
                    plane = plane_of(way, step)
                    z_copy(way, step, chunk, plane).wait_recv()
                    if chunk < main_count:
                        y_copy(way, step, chunk, plane * 2 + y).start()

                if step < planes - 1:

                    @pl.when(forwards(way, step))
                    def _(way=way, chunk=chunk):
                        z_copy(way, step + 1, chunk, plane_of(way, step)).start()

        for way in range(2):

            @pl.when(arrives(way, step))
            def _(way=way):
                owner = plane_of(way, step) * 2 + y
                arrived(owner)

        if step == 1:
            own_copy(1, partner).wait_recv()
            own_copy(2, partner).wait_recv()
            arrived(partner)
        else:
            across(step - 1)
    across(planes - 1)

    total_copy = n_copy(total, total_got, 1)
    total_copy.start()
    total_copy.wait_recv()
    whole = total[...] + total_got[...]
    for owner in range(wide_count):
        spread[:, owner * slab : (owner + 1) * slab] = jnp.where(
            code_ref[...] == owner, whole, jnp.float32(0.0)
        ).astype(jnp.bfloat16)
    base_copy.wait_recv()

    def finish(i, carry):
        columns = pl.ds(pl.multiple_of(i * slab, slab), slab)
        right = upv[:, :, columns].reshape(wide_count * slab, slab)
        adapted = jnp.dot(spread[...], right, preferred_element_type=jnp.float32)
        value = part[half + i] + got[i] + adapted
        out_ref[:, columns] = value.astype(jnp.bfloat16)
        return carry

    lax.fori_loop(0, half, finish, 0)

    base_copy.wait_send()
    total_copy.wait_send()
    for which in range(3):
        own_copy(which, me).wait_send()
    for step in range(1, planes):
        for way in range(2):
            sends = can_send(way) if step == 1 else forwards(way, step - 1)

            @pl.when(sends)
            def _(way=way, step=step):
                for chunk in range(len(chunks) + 1):
                    z_copy(way, step, chunk, plane_of(way, step - 1)).wait_send()

            @pl.when(arrives(way, step))
            def _(way=way, step=step):
                for chunk in range(main_count):
                    y_copy(way, step, chunk, plane_of(way, step) * 2 + y).wait_send()


def local(
    tokens,
    key_value_weight,
    adapter_down_weight,
    adapter_up_weight,
    token_adapter_index,
    adapter_rank_list,
):
    wide_count = lax.axis_size("wide")
    narrow_count = lax.axis_size("narrow")
    narrow_index = lax.axis_index("narrow")
    rows, depth = tokens.shape
    local_count, rank_limit, width = adapter_up_weight.shape
    columns = local_count * rank_limit
    part = width // narrow_count
    depth_slabs = depth // columns
    part_slabs = part // columns
    sub = 16
    down_slabs = columns // sub
    planes = wide_count // 2

    up = lax.dynamic_slice_in_dim(adapter_up_weight, narrow_index * part, part, 2)
    rank = adapter_rank_list[:, None]
    kept = jnp.arange(rank_limit, dtype=jnp.int32)[None, :] < rank
    scale = jnp.where(kept, ALPHA / rank.astype(jnp.float32), jnp.float32(0.0))
    up = (up.astype(jnp.float32) * scale[:, :, None]).astype(jnp.bfloat16)
    up = up.reshape(columns, part)
    down = adapter_down_weight.transpose(1, 2, 0).reshape(down_slabs, sub, depth)
    column_adapter = jnp.arange(columns, dtype=jnp.int32) // rank_limit
    code = jnp.where(
        (token_adapter_index % local_count)[:, None] == column_adapter[None, :],
        (token_adapter_index // local_count)[:, None],
        -1,
    )

    any_space = pl.BlockSpec(memory_space=pl.ANY)
    vmem = pl.BlockSpec(memory_space=pltpu.VMEM)
    dma = pltpu.SemaphoreType.DMA
    out, _, _ = pl.pallas_call(
        functools.partial(kernel, wide_count),
        out_shape=(
            jax.ShapeDtypeStruct((rows, part), jnp.bfloat16),
            jax.ShapeDtypeStruct((wide_count, down_slabs, sub, depth), jnp.bfloat16),
            jax.ShapeDtypeStruct((wide_count, columns, part), jnp.bfloat16),
        ),
        in_specs=[any_space, any_space, any_space, any_space, vmem],
        out_specs=(vmem, any_space, any_space),
        scratch_shapes=[
            pltpu.VMEM((rows, depth), jnp.bfloat16),
            pltpu.VMEM((2, depth_slabs, columns, columns), jnp.bfloat16),
            pltpu.VMEM((down_slabs, sub, depth), jnp.bfloat16),
            pltpu.VMEM((2 * part_slabs, rows, columns), jnp.float32),
            pltpu.VMEM((part_slabs, rows, columns), jnp.float32),
            pltpu.VMEM((wide_count, columns, part), jnp.bfloat16),
            pltpu.VMEM((rows, columns), jnp.float32),
            pltpu.VMEM((rows, columns), jnp.float32),
            pltpu.VMEM((rows, wide_count * columns), jnp.bfloat16),
            dma,
            dma((2,)),
            dma,
            dma((2, planes - 1, 6)),
            dma((2, planes - 1, 6)),
            dma((2, planes - 1, 4)),
            dma((2, planes - 1, 4)),
            dma((3,)),
            dma((3,)),
            dma((2,)),
            dma((2,)),
        ],
        compiler_params=pltpu.CompilerParams(
            collective_id=0, has_side_effects=True, vmem_limit_bytes=56 * 1024 * 1024
        ),
    )(tokens, key_value_weight.reshape(depth_slabs, columns, width), down, up, code)
    return out


def solution(mesh):
    in_specs = (
        P(("grp", "wide"), "narrow"),
        P("narrow", None),
        P("narrow", ("grp", "wide"), None),
        P(("grp", "wide"), None, None),
        P(("grp", "wide")),
        P(("grp", "wide")),
    )
    out_specs = P(("grp", "wide"), "narrow")
    return jax.shard_map(local, mesh=mesh, in_specs=in_specs, out_specs=out_specs, check_vma=False)
```
